128 devices in a mesh: rep: 8 (over y_hi, z), fsdp: 16 (over y_lo, x, core).
Axes of the slice: x: 4, y: 4 (y_hi: 2, y_lo: 2; y = y_hi * 2 + y_lo), z: 4, core: 2. Of those that a mesh axis runs over, the one named last changes fastest.
Arguments:
- token_ids: int32 [49152], P(('rep', 'fsdp')), may hold values from 0 to 128255, as said below
- normed_inputs: bfloat16 [49152, 8192], P(('rep', 'fsdp')), may hold values from -24 to 24
- kv_cotangent: bfloat16 [49152, 1024], P(('rep', 'fsdp')), may hold values from -0.5 to 0.5
- replica_weights: bfloat16 [8, 8192, 1024], P('rep', 'fsdp'), may hold values from -6 to 6
- snapshot: bfloat16 [8192, 1024], P('fsdp'), may hold values from -6 to 6
- momentum: float32 [8192, 1024], P('fsdp', 'rep'), may hold values from -4 to 4
Outputs:
- input_grad: float32 [49152, 8192], P(('rep', 'fsdp'))
- weight_grad: float32 [8, 8192, 1024], P('rep', 'fsdp')
- new_weights: float32 [8192, 1024], P('fsdp')
- new_momentum: float32 [8192, 1024], P('fsdp', 'rep')
The draws below stay inside these ranges and needn't reach their ends.
Inputs may be any that keep to these rules, and one draw needn't show every extreme that they name: `token_ids`: 0 is the padding id; it fills the end of each device's sequence of 384 tokens, and each sequence holds 96 or more other ids.
All inputs are finite; a program needn't handle non-finite values.
Results may differ from the reference program's by a relative error of at most 0.0003.
Values may be sent and summed in bfloat16 or wider, within the bound.
No kernel may reach another device: no remote copies, remote signals or barrier semaphores. Data moves between devices by JAX's collectives and lax.ppermute only.
A program may use at most 192 MiB of HBM per device.

```python
import jax
import jax.numpy as jnp
from jax import lax

D = 8192
VOCAB = 128256
TOK_DEV = 384
KV2 = 1024
TOKENS = 49152
N_REP = 8
N_FSDP = 16


def draw_token_ids(key, part):
    first_key, second_key = jax.random.split(jax.random.fold_in(key, 17))
    sequences = TOKENS // TOK_DEV
    lengths = jax.random.randint(first_key, (sequences, 1), TOK_DEV // 4, TOK_DEV + 1)
    values = jax.random.randint(second_key, (sequences, TOK_DEV), 1, VOCAB)
    places = jnp.arange(TOK_DEV)[None, :]
    return jnp.where(places < lengths, values, 0).reshape(TOKENS).astype(jnp.int32)


def spiked(drawn, stream_key, source, target, parts, factor):
    owner, partner = [(jnp.arange(drawn.shape[dim]) // (drawn.shape[dim] // parts)).reshape([-1 if axis == dim else 1 for axis in range(drawn.ndim)]) for dim in (source, target)]
    chosen = jax.random.permutation(stream_key, parts)[partner]
    strong = (owner == chosen) | (owner == (partner + parts // 2) % parts)
    return jnp.where(strong, factor * drawn, drawn)


def level_of(key, dims, shards, low, top_value):
    loudness = 1.0
    for axis_at, shards_of in shards:
        draws = jax.random.uniform(jax.random.fold_in(jax.random.fold_in(key, 6), axis_at), (shards_of,), jnp.float32, low / len(shards), top_value / len(shards))
        loudness = loudness * jnp.repeat(jnp.exp(draws), dims[axis_at] // shards_of).reshape((-1,) + (1,) * (len(dims) - 1 - axis_at))
    return loudness


def normal_values(own_key, dims, width, limit, cuts=(), held_as=jnp.bfloat16):
    factor_of = level_of(own_key, dims, cuts, -0.22, 0.18) if cuts else 1.0
    values = jax.random.normal(own_key, dims, jnp.float32) * width * factor_of
    return jnp.minimum(jnp.maximum(values, -limit), limit).astype(held_as)


def noise_with(rng, dims, width, limit, cuts, heavy, held_as=jnp.bfloat16):
    entries = width * jax.random.normal(rng, dims, jnp.float32)
    if cuts:
        entries = entries * level_of(rng, dims, cuts, -0.22, 0.18)
    return jnp.clip(spiked(entries, jax.random.fold_in(rng, 3), *heavy), -limit, limit).astype(held_as)


def setup_inputs(seed: int = 0) -> dict:
    keys = jax.random.split(jax.random.key(seed), 7)
    token_ids = draw_token_ids(jax.random.fold_in(keys[6], 71), 0)
    normed_inputs = noise_with(keys[1], (TOKENS, D), 1.0, 24.0, ((0, 128),), (0, 1, 128, 5.5))
    kv_cotangent = normal_values(keys[2], (TOKENS, KV2), (KV2 ** -0.5), 0.5, ((0, 128),))
    replica_weights = noise_with(keys[3], (N_REP, D, KV2), 1.0, 6.0, ((0, 8), (1, 16)), (0, 2, 8, 2.0))
    snapshot = normal_values(keys[4], (D, KV2), 1.0, 6.0, ((0, 16),))
    momentum = normal_values(keys[5], (D, KV2), 0.5, 4.0, ((0, 16), (1, 8)), jnp.float32)
    return {"token_ids": token_ids, "normed_inputs": normed_inputs, "kv_cotangent": kv_cotangent, "replica_weights": replica_weights, "snapshot": snapshot, "momentum": momentum}


outer_rate = 0.7
outer_beta = 0.9


def reference(token_ids, normed_inputs, kv_cotangent, replica_weights, snapshot, momentum):
    live_rows = (token_ids != 0).astype(jnp.bfloat16)[:, None]
    masked = kv_cotangent * live_rows
    inputs_grp = normed_inputs.reshape(N_REP, N_FSDP * TOK_DEV, D)
    cotan_grp = masked.reshape(N_REP, N_FSDP * TOK_DEV, KV2)

    def per_group(bundle):
        weights, inputs_one, cotan_one = bundle
        grad_inputs = jnp.dot(cotan_one, weights.T, preferred_element_type=jnp.float32)
        grad_weights = jnp.dot(inputs_one.T, cotan_one, preferred_element_type=jnp.float32)
        return grad_inputs, grad_weights

    grad_inputs, weight_grad = lax.map(per_group, (replica_weights, inputs_grp, cotan_grp))
    input_grad = grad_inputs.reshape(TOKENS, D)
    pseudo_grad = snapshot.astype(jnp.float32)[None] - replica_weights.astype(jnp.float32)
    outer_grad = jnp.sum(pseudo_grad, axis=0) / N_REP
    new_momentum = outer_beta * momentum + outer_grad
    new_weights = snapshot.astype(jnp.float32) - outer_rate * (outer_grad + outer_beta * new_momentum)
    return input_grad, weight_grad, new_weights, new_momentum
```

```python
import jax
import jax.numpy as jnp
from jax import lax
from jax.experimental import pallas as pl
from jax.experimental.pallas import tpu as pltpu
from jax.sharding import PartitionSpec as P

outer_rate = 0.7
outer_beta = 0.9
top_code = 32767.0
group_rows = 64
half = 256
MB = 1 << 20


def fsdp_index(y, x, c):
    return y * 8 + x * 2 + c


def moved(array, dy=0, dx=0, dc=0):
    pairs = []
    for y in range(2):
        for x in range(4):
            for c in range(2):
                pairs.append((fsdp_index(y, x, c), fsdp_index(y ^ dy, (x + dx) % 4, c ^ dc)))
    return lax.ppermute(array, "fsdp", pairs)


def moved_rep(array, dh=0, dz=0):
    pairs = [(h * 4 + z, (h ^ dh) * 4 + (z + dz) % 4) for h in range(2) for z in range(4)]
    return lax.ppermute(array, "rep", pairs)


def decoded(ref):
    rows = ref.shape[1] * group_rows // (group_rows + 1)
    codes = ref[0, :rows, :].astype(jnp.int32).astype(jnp.float32)
    unit = jnp.exp2(ref[0, rows:, :].astype(jnp.int32).astype(jnp.float32) * 0.25) * (1.0 / top_code)
    groups, width = unit.shape
    return (codes.reshape(groups, group_rows, width) * unit[:, None, :]).reshape(rows, width)


def store_coded(out_ref, total):
    rows, width = total.shape
    grouped = total.reshape(rows // group_rows, group_rows, width)
    peak = jnp.maximum(jnp.max(jnp.abs(grouped), axis=1), 1e-33)
    exponent = jnp.ceil(4.0 * jnp.log2(peak) + 0.01)
    scale = top_code / jnp.exp2(exponent * 0.25)
    codes = jnp.round(grouped * scale[:, None, :]).astype(jnp.int32).astype(jnp.int16)
    out_ref[0, :rows, :] = codes.reshape(rows, width)
    out_ref[0, rows:, :] = exponent.astype(jnp.int32).astype(jnp.int16)


def partial_kernel(n_adds, final, at_ref, mt_ref, own_ref, sib_ref, *refs):
    adds, out_ref = refs[:n_adds], refs[n_adds]
    tokens = jnp.concatenate([own_ref[...], sib_ref[...]], axis=0)
    total = jnp.dot(mt_ref[...], tokens, preferred_element_type=jnp.float32)
    for add in adds:
        total = total + decoded(add)
    if final:
        out_ref[...] = total.T
    else:
        store_coded(out_ref, total)


def partial_sums(mt, x_own, x_sib, own_at, sib_at, adds=(), final=False):
    n = len(own_at)
    rows = mt.shape[0]
    coded = rows + rows // group_rows
    at = jnp.stack([jnp.stack(own_at), jnp.stack(sib_at)] + [jnp.stack(place) for _, place in adds]).astype(jnp.int32)
    tokens = x_own.shape[0]
    specs = [
        pl.BlockSpec(mt.shape, lambda i, at: (0, 0)),
        pl.BlockSpec((tokens, half), lambda i, at: (0, at[0, i])),
        pl.BlockSpec((tokens, half), lambda i, at: (0, at[1, i])),
    ]
    for j in range(len(adds)):
        specs.append(pl.BlockSpec((1, coded, half), lambda i, at, j=j: (at[2 + j, i], 0, 0)))
    if final:
        out_spec = pl.BlockSpec((half, rows), lambda i, at: (i, 0))
        out_shape = jax.ShapeDtypeStruct((n * half, rows), jnp.float32)
    else:
        out_spec = pl.BlockSpec((1, coded, half), lambda i, at: (i, 0, 0))
        out_shape = jax.ShapeDtypeStruct((n, coded, half), jnp.int16)
    return pl.pallas_call(
        lambda *refs: partial_kernel(len(adds), final, *refs),
        grid_spec=pltpu.PrefetchScalarGridSpec(
            num_scalar_prefetch=1, grid=(n,), in_specs=specs, out_specs=out_spec
        ),
        out_shape=out_shape,
        compiler_params=pltpu.CompilerParams(vmem_limit_bytes=48 * MB),
        cost_estimate=pl.CostEstimate(
            flops=2 * n * rows * 2 * tokens * half,
            bytes_accessed=mt.size * 2 + n * half * (4 * tokens + (2 + 2 * len(adds)) * rows),
            transcendentals=0,
        ),
        name="partial_sums",
    )(at, mt, x_own, x_sib, *[array for array, _ in adds])


def columns_kernel(n, at_ref, masked_ref, *refs):
    step = pl.program_id(0)
    out_ref = refs[-1]
    for j in range(n):

        @pl.when(step == j)
        def _(piece=refs[j]):
            out_ref[...] = lax.dot_general(
                masked_ref[...], piece[...], (((1,), (1,)), ((), ())), preferred_element_type=jnp.float32
            )


def grad_columns(masked, pieces, places, wide, so_far):
    n = len(pieces)
    rows, features = pieces[0].shape
    tokens = masked.shape[0]
    at = jnp.stack(places).astype(jnp.int32)
    specs = [pl.BlockSpec(masked.shape, lambda i, at: (0, 0))]
    specs += [pl.BlockSpec((rows, features), lambda i, at: (0, 0))] * n
    operands = [at, masked, *pieces]
    aliases = {}
    if so_far is not None:
        specs.append(pl.BlockSpec(memory_space=pl.ANY))
        aliases = {len(operands): 0}
        operands.append(so_far)
    return pl.pallas_call(
        lambda *refs: columns_kernel(n, *refs),
        grid_spec=pltpu.PrefetchScalarGridSpec(
            num_scalar_prefetch=1,
            grid=(n,),
            in_specs=specs,
            out_specs=pl.BlockSpec((tokens, rows), lambda i, at: (0, at[i])),
        ),
        out_shape=jax.ShapeDtypeStruct((tokens, wide), jnp.float32),
        input_output_aliases=aliases,
        compiler_params=pltpu.CompilerParams(vmem_limit_bytes=48 * MB),
        cost_estimate=pl.CostEstimate(
            flops=2 * n * rows * tokens * features,
            bytes_accessed=n * rows * (2 * features + 4 * tokens) + masked.size * 2,
            transcendentals=0,
        ),
        name="grad_columns",
    )(*operands)


def outer_step(weights, snapshot, momentum):
    groups = lax.axis_size("rep")
    rep = lax.axis_index("rep")
    h, z = rep // 4, rep % 4
    rows, width = momentum.shape

    def by_owner(array):
        return array.reshape(rows, 2, 4, width).transpose(2, 1, 0, 3)

    w_cols = by_owner(weights)
    take = lambda array, i: lax.dynamic_index_in_dim(array, i, 0, keepdims=False)
    snap_z = take(by_owner(snapshot), z).astype(jnp.float32)
    total = snap_z - take(w_cols, z).astype(jnp.float32)
    for dz in (1, 3, 2):
        arrived = moved_rep(take(w_cols, (z + dz) % 4), dz=dz)
        total = total + (snap_z - arrived.astype(jnp.float32))
    outer_grad = (take(total, h) + moved_rep(take(total, 1 - h), dh=1)) / groups
    new_momentum = outer_beta * momentum + outer_grad
    new_part = take(snap_z, h) - outer_rate * (outer_grad + outer_beta * new_momentum)
    other = moved_rep(new_part, dh=1)
    pair = jnp.where(h == 0, jnp.stack([new_part, other]), jnp.stack([other, new_part]))
    out = jnp.zeros((4, 2, rows, width), jnp.float32)
    for dz in (0, 1, 3, 2):
        arrived = moved_rep(pair, dz=dz) if dz else pair
        out = lax.dynamic_update_index_in_dim(out, arrived, (z - dz) % 4, 0)
    new_weights = out.transpose(2, 1, 0, 3).reshape(rows, 8 * width)
    return new_weights, new_momentum


def per_device(token_ids, normed_inputs, kv_cotangent, replica_weights, snapshot, momentum):
    f = lax.axis_index("fsdp")
    y, x, c = f // 8, (f // 2) % 4, f % 2
    tokens, wide = normed_inputs.shape
    weights = replica_weights[0]
    block = weights.shape[0]

    live_rows = (token_ids != 0).astype(jnp.bfloat16)[:, None]
    masked = kv_cotangent * live_rows

    by_core = normed_inputs.reshape(tokens, 8, 2, block)
    for_other = lax.dynamic_index_in_dim(by_core, 1 - c, 2, keepdims=False).reshape(tokens, 8 * block)
    x_sib = moved(for_other, dc=1)
    masked_sib = moved(masked, dc=1)
    mt = jnp.concatenate([masked, masked_sib], axis=0).T

    def halves(dy_list, dx, h):
        own = [fsdp_index(yy, (x + dx) % 4, c) * 2 + h for yy in dy_list]
        sib = [(yy * 4 + (x + dx) % 4) * 2 + h for yy in dy_list]
        return own, sib

    zero, one = jnp.int32(0), jnp.int32(1)
    both = [zero, one]

    def coded(dx, h, adds=()):
        own, sib = halves(both, dx, h)
        return partial_sums(mt, normed_inputs, x_sib, own, sib, [(a, both) for a in adds])

    w_y = moved(weights, dy=1)
    w_r1 = moved(weights, dx=1)
    w_l1 = moved(weights, dx=-1)

    far_a = moved(coded(2, 0), dx=1)
    far_b = moved(coded(2, 1), dx=-1)
    left_b = moved(coded(1, 1), dx=1)
    right_a = moved(coded(-1, 0), dx=-1)
    left_a = moved(coded(1, 0, [far_a]), dx=1)
    right_b = moved(coded(-1, 1, [far_b]), dx=-1)

    def at_home(yy, extra, final):
        outs = []
        for h, got in ((0, (left_a, right_a)), (1, (left_b, right_b))):
            own, sib = halves([yy], 0, h)
            adds = [(a, [yy]) for a in got] + [(a, [zero]) for a in extra[h : h + 1]]
            outs.append(partial_sums(mt, normed_inputs, x_sib, own, sib, adds, final))
        return outs

    from_y = [moved(a, dy=1) for a in at_home(1 - y, (), False)]
    weight_grad = jnp.concatenate(at_home(y, from_y, True), axis=0)

    w_r1y = moved(w_y, dx=1)
    w_l1y = moved(w_y, dx=-1)
    w_r2 = moved(w_r1[:half], dx=1)
    w_l2 = moved(w_l1[half:], dx=-1)
    w_r2y = moved(w_r1y[:half], dx=1)
    w_l2y = moved(w_l1y[half:], dx=-1)

    def place(dy, dx, dc):
        return fsdp_index(y ^ dy, (x + dx) % 4, c ^ dc)

    def with_other(pieces, places):
        return pieces + [moved(p, dc=1) for p in pieces], [place(*p, 0) for p in places] + [place(*p, 1) for p in places]

    grad = None
    for pieces, places in (
        ([weights, w_y], [(0, 0), (1, 0)]),
        ([w_r1, w_l1], [(0, -1), (0, 1)]),
        ([w_r1y, w_l1y], [(1, -1), (1, 1)]),
    ):
        grad = grad_columns(masked, *with_other(pieces, places), wide, grad)
    pieces = [w_r2, w_l2, w_r2y, w_l2y]
    at = [place(dy, 2, dc) * 2 + h for dc in range(2) for dy in range(2) for h in range(2)]
    input_grad = grad_columns(masked, pieces + [moved(p, dc=1) for p in pieces], at, wide, grad)

    new_weights, new_momentum = outer_step(weights, snapshot, momentum)
    return input_grad, weight_grad[None], new_weights, new_momentum


def solution(mesh):
    return jax.shard_map(
        per_device,
        mesh=mesh,
        in_specs=(
            P(("rep", "fsdp")),
            P(("rep", "fsdp"), None),
            P(("rep", "fsdp"), None),
            P("rep", "fsdp", None),
            P("fsdp", None),
            P("fsdp", "rep"),
        ),
        out_specs=(
            P(("rep", "fsdp"), None),
            P("rep", "fsdp", None),
            P("fsdp", None),
            P("fsdp", "rep"),
        ),
        check_vma=False,
    )
```

```python
import jax
import jax.numpy as jnp
import numpy as np
from jax import lax
from jax.experimental import pallas as pl
from jax.experimental.pallas import tpu as pltpu
from jax.sharding import PartitionSpec as P

outer_rate = 0.7
outer_beta = 0.9
top_code = 32767.0
group_rows = 32
half = 256
MB = 1 << 20
vmem = 60 * MB
tiny = pl.CostEstimate(flops=1000, bytes_accessed=1000, transcendentals=0)


def fsdp_index(y, x, c):
    return y * 8 + x * 2 + c


def decoded(ref):
    rows = ref.shape[1] * group_rows // (group_rows + 1)
    codes = ref[0, :rows, :].astype(jnp.int32).astype(jnp.float32)
    unit = jnp.exp2(ref[0, rows:, :].astype(jnp.int32).astype(jnp.float32) * 0.25) * (1.0 / top_code)
    groups, width = unit.shape
    return (codes.reshape(groups, group_rows, width) * unit[:, None, :]).reshape(rows, width)


def store_coded(out_ref, total):
    rows, width = total.shape
    grouped = total.reshape(rows // group_rows, group_rows, width)
    peak = jnp.maximum(jnp.max(jnp.abs(grouped), axis=1), 1e-33)
    exponent = jnp.ceil(4.0 * jnp.log2(peak) + 0.01)
    scale = top_code / jnp.exp2(exponent * 0.25)
    codes = jnp.round(grouped * scale[:, None, :]).astype(jnp.int32).astype(jnp.int16)
    out_ref[0, :rows, :] = codes.reshape(rows, width)
    out_ref[0, rows:, :] = exponent.astype(jnp.int32).astype(jnp.int16)


def sums_kernel(groups, n_adds, at_ref, mt_ref, own_ref, sib_ref, *refs):
    step = pl.program_id(0)
    adds, outs = refs[:n_adds], refs[-len(groups) :]
    first = 0
    for (count, used, final), out_ref in zip(groups, outs, strict=True):

        @pl.when((step >= first) & (step < first + count))
        def _(used=used, final=final, out_ref=out_ref):
            tokens = jnp.concatenate([own_ref[...], sib_ref[...]], axis=0)
            total = jnp.dot(mt_ref[...], tokens, preferred_element_type=jnp.float32)
            for j in used:
                total = total + decoded(adds[j])
            if final:
                out_ref[...] = total.T
            else:
                store_coded(out_ref, total)

        first += count


def sums(at, offset, mt, x_own, x_sib, groups, adds=(), final_at=0):
    rows, both_tokens = mt.shape
    tokens = both_tokens // 2
    coded = rows + rows // group_rows
    specs = [
        pl.BlockSpec(mt.shape, lambda i, at: (0, 0)),
        pl.BlockSpec((tokens, half), lambda i, at: (0, at[offset + i])),
        pl.BlockSpec((tokens, half), lambda i, at: (0, at[offset + i])),
    ]
    for _, index in adds:
        specs.append(pl.BlockSpec((1, coded, half), lambda i, at, index=index: (index(i, at), 0, 0)))
    out_specs, out_shapes, first = [], [], 0
    for count, _, final in groups:
        if final:
            out_specs.append(pl.BlockSpec((half, rows), lambda i, at: (at[final_at], 0)))
            out_shapes.append(jax.ShapeDtypeStruct((2 * half, rows), jnp.float32))
        else:
            out_specs.append(
                pl.BlockSpec(
                    (1, coded, half),
                    lambda i, at, first=first, count=count: (jnp.clip(i - first, 0, count - 1), 0, 0),
                )
            )
            out_shapes.append(jax.ShapeDtypeStruct((count, coded, half), jnp.int16))
        first += count
    return pl.pallas_call(
        lambda *refs: sums_kernel(groups, len(adds), *refs),
        grid_spec=pltpu.PrefetchScalarGridSpec(
            num_scalar_prefetch=1, grid=(first,), in_specs=specs, out_specs=out_specs
        ),
        out_shape=out_shapes,
        compiler_params=pltpu.CompilerParams(vmem_limit_bytes=vmem),
        cost_estimate=tiny,
        name="partial_sums",
    )(at, mt, x_own, x_sib, *[array for array, _ in adds])


def last_kernel(at_ref, add_ref, _, out_ref):
    out_ref[...] = decoded(add_ref).T


def last_rows(at, offset, coded, so_far):
    return pl.pallas_call(
        last_kernel,
        grid_spec=pltpu.PrefetchScalarGridSpec(
            num_scalar_prefetch=1,
            grid=(1,),
            in_specs=[pl.BlockSpec(coded.shape, lambda i, at: (0, 0, 0)), pl.BlockSpec(memory_space=pl.ANY)],
            out_specs=pl.BlockSpec((half, so_far.shape[1]), lambda i, at: (at[offset], 0)),
        ),
        out_shape=jax.ShapeDtypeStruct(so_far.shape, so_far.dtype),
        input_output_aliases={2: 0},
        compiler_params=pltpu.CompilerParams(vmem_limit_bytes=vmem),
        cost_estimate=tiny,
        name="last_rows",
    )(at, coded, so_far)


def columns_kernel(n, at_ref, masked_ref, *refs):
    step = pl.program_id(0)
    out_ref = refs[-1]
    for j in range(n):

        @pl.when(step == j)
        def _(piece=refs[j]):
            out_ref[...] = lax.dot_general(
                masked_ref[...], piece[...], (((1,), (1,)), ((), ())), preferred_element_type=jnp.float32
            )


def grad_columns(at, offset, masked, pieces, wide, so_far, rows):
    n = len(pieces)
    features = pieces[0][0].shape[1]
    tokens = masked.shape[0]
    specs = [pl.BlockSpec(masked.shape, lambda i, at: (0, 0))]
    specs += [pl.BlockSpec((rows, features), lambda i, at, k=k: (k, 0)) for _, k in pieces]
    operands = [at, masked, *[array for array, _ in pieces]]
    aliases = {}
    if so_far is not None:
        specs.append(pl.BlockSpec(memory_space=pl.ANY))
        aliases = {len(operands): 0}
        operands.append(so_far)
    return pl.pallas_call(
        lambda *refs: columns_kernel(n, *refs),
        grid_spec=pltpu.PrefetchScalarGridSpec(
            num_scalar_prefetch=1,
            grid=(n,),
            in_specs=specs,
            out_specs=pl.BlockSpec((tokens, rows), lambda i, at: (0, at[offset + i])),
        ),
        out_shape=jax.ShapeDtypeStruct((tokens, wide), jnp.float32),
        input_output_aliases=aliases,
        compiler_params=pltpu.CompilerParams(vmem_limit_bytes=vmem),
        cost_estimate=tiny,
        name="grad_columns",
    )(*operands)


def assemble_kernel(at_ref, *refs):
    step = pl.program_id(0)
    out_ref = refs[-1]
    for j in range(4):
        for k in range(2):

            @pl.when(step == 2 * j + k)
            def _(piece=refs[j], k=k):
                rows = out_ref.shape[0]
                out_ref[...] = piece[k * rows : (k + 1) * rows, :]


def assembled(pieces, places):
    rows, width = pieces[0].shape
    return pl.pallas_call(
        assemble_kernel,
        grid_spec=pltpu.PrefetchScalarGridSpec(
            num_scalar_prefetch=1,
            grid=(8,),
            in_specs=[pl.BlockSpec((rows, width), lambda i, at: (0, 0))] * 4,
            out_specs=pl.BlockSpec((rows // 2, width), lambda i, at: (0, at[i])),
        ),
        out_shape=jax.ShapeDtypeStruct((rows // 2, 8 * width), jnp.float32),
        compiler_params=pltpu.CompilerParams(vmem_limit_bytes=vmem),
        cost_estimate=tiny,
        name="assembled",
    )(places, *pieces)


def group_columns(array, zz, h, width):
    cut = lambda hh: lax.dynamic_slice_in_dim(array, (hh * 4 + zz) * width, width, 1)
    return jnp.concatenate([cut(h), cut(1 - h)], axis=0)


def together(*arrays):
    return lax.optimization_barrier(arrays)


def sent(array, pairs):
    return lax.ppermute(array, "fsdp", pairs)


def sent_rep(array, dh=0, dz=0):
    pairs = [(h * 4 + z, (h ^ dh) * 4 + (z + dz) % 4) for h in range(2) for z in range(4)]
    return lax.ppermute(array, "rep", pairs)


chips = [(y, x, c) for y in range(2) for x in range(4) for c in range(2)]
to_core = [(fsdp_index(y, x, c), fsdp_index(y, x, 1 - c)) for y, x, c in chips]
to_y = [(fsdp_index(y, x, c), fsdp_index(1 - y, x, c)) for y, x, c in chips]
ahead = [(fsdp_index(y, x, c), fsdp_index(y, (x + 1 - 2 * c) % 4, c)) for y, x, c in chips]
behind = [(fsdp_index(y, x, c), fsdp_index(y, (x - 1 + 2 * c) % 4, c)) for y, x, c in chips]


def tables():
    starts, rows = {}, []
    for me in range(16):
        y, x, c = me // 8, (me // 2) % 4, me % 2
        s, o, row = 1 - 2 * c, 1 - c, []

        def cols(yy, dx):
            return [fsdp_index(yy, (x + dx) % 4, cc) * 2 + c for cc in range(2)]

        def places(*pieces):
            return [fsdp_index(y ^ dy, (x + dx) % 4, cc) for dy, dx, cc in pieces]

        for name, entries in (
            ("first", cols(1 - y, 2) + cols(y, -s) + cols(1 - y, -s) + cols(1 - y, s)),
            ("far", cols(y, 2)),
            ("near", cols(y, s) + cols(1 - y, 0)),
            ("home", [fsdp_index(y, x, cc) * 2 + c for cc in (o, c)]),
            ("cores", [o, c]),
            ("grad1", places((0, 0, c), (0, 0, o), (0, -s, c), (0, -s, o))),
            ("grad2", places((0, s, o), (0, s, c), (1, 0, c), (1, 0, o))),
            ("grad3", places((0, 2, c), (0, 2, o), (1, 2, c))),
            ("grad4", places((1, 2, o), (1, -s, c), (1, -s, o), (1, s, o), (1, s, c))),
        ):
            starts[name] = len(row)
            row += entries
        rows.append(row)
    rep_rows = []
    for me in range(8):
        h, z = me // 4, me % 4
        rep_rows.append([hh * 4 + (z - dz) % 4 for dz in (0, 1, 3, 2) for hh in (h, 1 - h)])
    return starts, np.array(rows, np.int32), np.array(rep_rows, np.int32)


def per_device(token_ids, normed_inputs, kv_cotangent, replica_weights, snapshot, momentum):
    wide = normed_inputs.shape[1]
    w = replica_weights[0]
    block = w.shape[0]
    groups = lax.axis_size("rep")
    rep = lax.axis_index("rep")
    gh, gz = rep // 4, rep % 4
    rows, width = momentum.shape
    starts, table, rep_table = tables()
    at = lax.dynamic_index_in_dim(jnp.asarray(table), lax.axis_index("fsdp"), 0, keepdims=False)
    rep_at = lax.dynamic_index_in_dim(jnp.asarray(rep_table), rep, 0, keepdims=False)

    def columns(name, pieces, so_far):
        return grad_columns(at, starts[name], masked, pieces, wide, so_far, block)

    def part_sums(name, *args, **kw):
        return sums(at, starts[name], mt, normed_inputs, x_sib, *args, **kw)

    x_sib = sent(normed_inputs, to_core)
    live_rows = (token_ids != 0).astype(jnp.bfloat16)[:, None]
    masked = kv_cotangent * live_rows
    masked_sib = sent(masked, to_core)
    both = jnp.concatenate([w, sent(w, to_core)], axis=0)
    f, v = sent(both, ahead), sent(w, to_y)
    mt = jnp.concatenate([masked, masked_sib], axis=0).T
    z1, z3, z2 = (sent_rep(group_columns(w, (gz + dz) % 4, gh, width), dz=dz) for dz in (1, 3, 2))
    far_y, b, near_o = part_sums("first", [(2, [], False), (4, [], False), (2, [], False)])
    both, f, v, far_y, b, near_o, z1, z3, z2, mt = together(both, f, v, far_y, b, near_o, z1, z3, z2, mt)

    b, f3, far_y = sent(b, behind), sent(f[:block], ahead), sent(far_y, to_y)
    d, v_s = sent(f, to_core), sent(v, to_core)
    snap = group_columns(snapshot, gz, gh, width).astype(jnp.float32)
    total = snap - group_columns(both[:block], gz, gh, width).astype(jnp.float32)
    for part in (z1, z3, z2):
        total = total + (snap - part.astype(jnp.float32))
    total_in = sent_rep(total[rows:], dh=1)
    grad = columns("grad1", [(both, 0), (both, 1), (f, 0), (f, 1)], None)
    v_both = jnp.concatenate([v, v_s], axis=0)
    (far,) = part_sums("far", [(2, [0], False)], [(far_y, lambda i, at: i)])
    b, f3, d, v_both, total, total_in, grad, far, near_o, mt = together(
        b, f3, d, v_both, total, total_in, grad, far, near_o, mt
    )

    far, near_o, h = sent(far, ahead), sent(near_o, ahead), sent(f3, to_y)
    d3 = sent(f3, to_core)
    outer_grad = (total[:rows] + total_in) / groups
    new_momentum = outer_beta * momentum + outer_grad
    new_part = snap[:rows] - outer_rate * (outer_grad + outer_beta * new_momentum)
    part_in = sent_rep(new_part, dh=1)
    grad = columns("grad2", [(d, 0), (d, 1), (v_both, 0), (v_both, 1)], grad)
    near, home_o = part_sums(
        "near",
        [(2, [0], False), (2, [1, 2], False)],
        [
            (far, lambda i, at: jnp.clip(i, 0, 1)),
            (b, lambda i, at: jnp.clip(i, 2, 3)),
            (near_o, lambda i, at: jnp.clip(i - 2, 0, 1)),
        ],
    )
    near, home_o, h, f3, d3, v_both, b, new_momentum, new_part, part_in, grad, mt = together(
        near, home_o, h, f3, d3, v_both, b, new_momentum, new_part, part_in, grad, mt
    )

    near, g, from_y = sent(near, ahead), sent(v_both, ahead), sent(home_o, to_y)
    part = jnp.concatenate([new_part, part_in], axis=0)
    z1, z3 = sent_rep(part, dz=1), sent_rep(part, dz=3)
    grad = columns("grad3", [(f3, 0), (d3, 0), (h, 0)], grad)
    by_core = [(array, lambda i, at: at[starts["cores"] + i]) for array in (b, near, from_y)]
    for_other, weight_grad = part_sums(
        "home", [(1, [0, 1, 2], False), (1, [0, 1, 2], True)], by_core, final_at=starts["cores"] + 1
    )
    h, g, part, z1, z3, grad, for_other, weight_grad = together(h, g, part, z1, z3, grad, for_other, weight_grad)

    from_other, e, h_s = sent(for_other, to_core), sent(g, to_core), sent(h, to_core)
    z2 = jnp.concatenate([sent_rep(z1[:rows], dz=1), sent_rep(z3[rows:], dz=3)], axis=0)
    weight_grad = last_rows(at, starts["cores"], from_other, weight_grad)
    input_grad = columns("grad4", [(h_s, 0), (g, 0), (g, 1), (e, 0), (e, 1)], grad)
    rep_at, _ = together(rep_at, input_grad)
    new_weights = assembled([part, z1, z3, z2], rep_at)
    return input_grad, weight_grad[None], new_weights, new_momentum


def solution(mesh):
    return jax.shard_map(
        per_device,
        mesh=mesh,
        in_specs=(
            P(("rep", "fsdp")),
            P(("rep", "fsdp"), None),
            P(("rep", "fsdp"), None),
            P("rep", "fsdp", None),
            P("fsdp", None),
            P("fsdp", "rep"),
        ),
        out_specs=(
            P(("rep", "fsdp"), None),
            P("rep", "fsdp", None),
            P("fsdp", None),
            P("fsdp", "rep"),
        ),
        check_vma=False,
    )
```

```python
import jax
import jax.numpy as jnp
import numpy as np
from jax import lax
from jax.experimental import pallas as pl
from jax.experimental.pallas import tpu as pltpu
from jax.sharding import PartitionSpec as P

outer_rate = 0.7
outer_beta = 0.9
top_code = 32767.0
group_rows = 32
half = 256
MB = 1 << 20
vmem = 60 * MB
tiny = pl.CostEstimate(flops=1000, bytes_accessed=1000, transcendentals=0)


def fsdp_index(y, x, c):
    return y * 8 + x * 2 + c


def decoded(ref):
    rows = ref.shape[1] * group_rows // (group_rows + 1)
    codes = ref[0, :rows, :].astype(jnp.int32).astype(jnp.float32)
    unit = jnp.exp2(ref[0, rows:, :].astype(jnp.int32).astype(jnp.float32) * 0.25) * (1.0 / top_code)
    groups, width = unit.shape
    return (codes.reshape(groups, group_rows, width) * unit[:, None, :]).reshape(rows, width)


def store_coded(out_ref, total):
    rows, width = total.shape
    grouped = total.reshape(rows // group_rows, group_rows, width)
    peak = jnp.maximum(jnp.max(jnp.abs(grouped), axis=1), 1e-33)
    exponent = jnp.ceil(4.0 * jnp.log2(peak) + 0.01)
    scale = top_code / jnp.exp2(exponent * 0.25)
    codes = jnp.round(grouped * scale[:, None, :]).astype(jnp.int32).astype(jnp.int16)
    out_ref[0, :rows, :] = codes.reshape(rows, width)
    out_ref[0, rows:, :] = exponent.astype(jnp.int32).astype(jnp.int16)


def sums_kernel(groups, n_adds, at_ref, mt_ref, own_ref, sib_ref, *refs):
    step = pl.program_id(0)
    adds, outs = refs[:n_adds], refs[-len(groups) :]
    first = 0
    for (count, used, final), out_ref in zip(groups, outs, strict=True):

        @pl.when((step >= first) & (step < first + count))
        def _(used=used, final=final, out_ref=out_ref):
            tokens = jnp.concatenate([own_ref[...], sib_ref[...]], axis=0)
            total = jnp.dot(mt_ref[...], tokens, preferred_element_type=jnp.float32)
            for j in used:
                total = total + decoded(adds[j])
            if final:
                out_ref[...] = total.T
            else:
                store_coded(out_ref, total)

        first += count


def sums(at, offset, mt, x_own, x_sib, groups, adds=(), final_at=0):
    rows, both_tokens = mt.shape
    tokens = both_tokens // 2
    coded = rows + rows // group_rows
    specs = [
        pl.BlockSpec(mt.shape, lambda i, at: (0, 0)),
        pl.BlockSpec((tokens, half), lambda i, at: (0, at[offset + i])),
        pl.BlockSpec((tokens, half), lambda i, at: (0, at[offset + i])),
    ]
    for _, index in adds:
        specs.append(pl.BlockSpec((1, coded, half), lambda i, at, index=index: (index(i, at), 0, 0)))
    out_specs, out_shapes, first = [], [], 0
    for count, _, final in groups:
        if final:
            out_specs.append(pl.BlockSpec((half, rows), lambda i, at: (at[final_at], 0)))
            out_shapes.append(jax.ShapeDtypeStruct((2 * half, rows), jnp.float32))
        else:
            out_specs.append(
                pl.BlockSpec(
                    (1, coded, half),
                    lambda i, at, first=first, count=count: (jnp.clip(i - first, 0, count - 1), 0, 0),
                )
            )
            out_shapes.append(jax.ShapeDtypeStruct((count, coded, half), jnp.int16))
        first += count
    return pl.pallas_call(
        lambda *refs: sums_kernel(groups, len(adds), *refs),
        grid_spec=pltpu.PrefetchScalarGridSpec(
            num_scalar_prefetch=1, grid=(first,), in_specs=specs, out_specs=out_specs
        ),
        out_shape=out_shapes,
        compiler_params=pltpu.CompilerParams(vmem_limit_bytes=vmem),
        cost_estimate=tiny,
        name="partial_sums",
    )(at, mt, x_own, x_sib, *[array for array, _ in adds])


def last_kernel(at_ref, add_ref, _, out_ref):
    out_ref[...] = decoded(add_ref).T


def last_rows(at, offset, coded, so_far):
    return pl.pallas_call(
        last_kernel,
        grid_spec=pltpu.PrefetchScalarGridSpec(
            num_scalar_prefetch=1,
            grid=(1,),
            in_specs=[pl.BlockSpec(coded.shape, lambda i, at: (0, 0, 0)), pl.BlockSpec(memory_space=pl.ANY)],
            out_specs=pl.BlockSpec((half, so_far.shape[1]), lambda i, at: (at[offset], 0)),
        ),
        out_shape=jax.ShapeDtypeStruct(so_far.shape, so_far.dtype),
        input_output_aliases={2: 0},
        compiler_params=pltpu.CompilerParams(vmem_limit_bytes=vmem),
        cost_estimate=tiny,
        name="last_rows",
    )(at, coded, so_far)


def columns_kernel(n, at_ref, masked_ref, *refs):
    step = pl.program_id(0)
    out_ref = refs[-1]
    for j in range(n):

        @pl.when(step == j)
        def _(piece=refs[j]):
            out_ref[...] = lax.dot_general(
                masked_ref[...], piece[...], (((1,), (1,)), ((), ())), preferred_element_type=jnp.float32
            )


def grad_columns(at, offset, masked, pieces, wide, so_far, rows):
    n = len(pieces)
    features = pieces[0][0].shape[1]
    tokens = masked.shape[0]
    specs = [pl.BlockSpec(masked.shape, lambda i, at: (0, 0))]
    specs += [pl.BlockSpec((rows, features), lambda i, at, k=k: (k, 0)) for _, k in pieces]
    operands = [at, masked, *[array for array, _ in pieces]]
    aliases = {}
    if so_far is not None:
        specs.append(pl.BlockSpec(memory_space=pl.ANY))
        aliases = {len(operands): 0}
        operands.append(so_far)
    return pl.pallas_call(
        lambda *refs: columns_kernel(n, *refs),
        grid_spec=pltpu.PrefetchScalarGridSpec(
            num_scalar_prefetch=1,
            grid=(n,),
            in_specs=specs,
            out_specs=pl.BlockSpec((tokens, rows), lambda i, at: (0, at[offset + i])),
        ),
        out_shape=jax.ShapeDtypeStruct((tokens, wide), jnp.float32),
        input_output_aliases=aliases,
        compiler_params=pltpu.CompilerParams(vmem_limit_bytes=vmem),
        cost_estimate=tiny,
        name="grad_columns",
    )(*operands)


def assemble_kernel(at_ref, *refs):
    out_ref = refs[-1]
    for k, piece in enumerate(refs[:-1]):
        width = piece.shape[1]
        out_ref[:, pl.ds(pl.multiple_of(at_ref[k] * width, width), width)] = piece[...]


def assembled(pieces, places):
    both_rows, width = pieces[0].shape
    rows, steps = both_rows // 2, 4
    tile = rows // steps
    return pl.pallas_call(
        assemble_kernel,
        grid_spec=pltpu.PrefetchScalarGridSpec(
            num_scalar_prefetch=1,
            grid=(steps,),
            in_specs=[pl.BlockSpec((tile, width), lambda i, at, k=k: (k * steps + i, 0)) for _ in pieces for k in range(2)],
            out_specs=pl.BlockSpec((tile, 8 * width), lambda i, at: (i, 0)),
        ),
        out_shape=jax.ShapeDtypeStruct((rows, 8 * width), jnp.float32),
        compiler_params=pltpu.CompilerParams(vmem_limit_bytes=vmem),
        cost_estimate=tiny,
        name="assembled",
    )(places, *[piece for piece in pieces for _ in range(2)])


def group_columns(array, zz, h, width):
    cut = lambda hh: lax.dynamic_slice_in_dim(array, (hh * 4 + zz) * width, width, 1)
    return jnp.concatenate([cut(h), cut(1 - h)], axis=0)


def together(*arrays):
    return lax.optimization_barrier(arrays)


def sent(array, pairs):
    return lax.ppermute(array, "fsdp", pairs)


def sent_rep(array, dh=0, dz=0):
    pairs = [(h * 4 + z, (h ^ dh) * 4 + (z + dz) % 4) for h in range(2) for z in range(4)]
    return lax.ppermute(array, "rep", pairs)


chips = [(y, x, c) for y in range(2) for x in range(4) for c in range(2)]
to_core = [(fsdp_index(y, x, c), fsdp_index(y, x, 1 - c)) for y, x, c in chips]
to_y = [(fsdp_index(y, x, c), fsdp_index(1 - y, x, c)) for y, x, c in chips]
ahead = [(fsdp_index(y, x, c), fsdp_index(y, (x + 1 - 2 * c) % 4, c)) for y, x, c in chips]
behind = [(fsdp_index(y, x, c), fsdp_index(y, (x - 1 + 2 * c) % 4, c)) for y, x, c in chips]


def tables():
    starts, rows = {}, []
    for me in range(16):
        y, x, c = me // 8, (me // 2) % 4, me % 2
        s, o, row = 1 - 2 * c, 1 - c, []

        def cols(yy, dx):
            return [fsdp_index(yy, (x + dx) % 4, cc) * 2 + c for cc in range(2)]

        def places(*pieces):
            return [fsdp_index(y ^ dy, (x + dx) % 4, cc) for dy, dx, cc in pieces]

        for name, entries in (
            ("first", cols(1 - y, 2) + cols(y, -s) + cols(1 - y, -s) + cols(1 - y, s)),
            ("far", cols(y, 2)),
            ("near", cols(y, s) + cols(1 - y, 0)),
            ("home", [fsdp_index(y, x, cc) * 2 + c for cc in (o, c)]),
            ("cores", [o, c]),
            ("grad1", places((0, 0, c), (0, 0, o), (0, -s, c), (0, -s, o))),
            ("grad2", places((0, s, o), (0, s, c), (1, 0, c), (1, 0, o))),
            ("grad3", places((0, 2, c), (0, 2, o), (1, 2, c), (1, -s, c), (1, s, o))),
            ("grad4", places((1, 2, o), (1, -s, o), (1, s, c))),
        ):
            starts[name] = len(row)
            row += entries
        rows.append(row)
    rep_rows = []
    for me in range(8):
        h, z = me // 4, me % 4
        rep_rows.append([hh * 4 + (z - dz) % 4 for dz in (0, 1, 3, 2) for hh in (h, 1 - h)])
    return starts, np.array(rows, np.int32), np.array(rep_rows, np.int32)


def per_device(token_ids, normed_inputs, kv_cotangent, replica_weights, snapshot, momentum):
    wide = normed_inputs.shape[1]
    w = replica_weights[0]
    block = w.shape[0]
    groups = lax.axis_size("rep")
    rep = lax.axis_index("rep")
    gh, gz = rep // 4, rep % 4
    rows, width = momentum.shape
    starts, table, rep_table = tables()
    at = lax.dynamic_index_in_dim(jnp.asarray(table), lax.axis_index("fsdp"), 0, keepdims=False)
    rep_at = lax.dynamic_index_in_dim(jnp.asarray(rep_table), rep, 0, keepdims=False)

    def columns(name, pieces, so_far):
        return grad_columns(at, starts[name], masked, pieces, wide, so_far, block)

    def part_sums(name, *args, **kw):
        return sums(at, starts[name], mt, normed_inputs, x_sib, *args, **kw)

    x_sib = sent(normed_inputs, to_core)
    f1, v, w_s = sent(w, ahead), sent(w, to_y), sent(w, to_core)
    live_rows = (token_ids != 0).astype(jnp.bfloat16)[:, None]
    masked = kv_cotangent * live_rows
    masked_sib = sent(masked, to_core)
    mt = jnp.concatenate([masked, masked_sib], axis=0).T
    w_z, masked_sib, w_s = together(w, masked_sib, w_s)
    c1, c2, c3 = (group_columns(w_z, (gz + dz) % 4, gh, width) for dz in (1, 2, 3))
    w_later, f1, mt, at, rep_at, c1, c2, c3 = together(w_s, f1, mt, at, rep_at, c1, c2, c3)
    f2 = sent(w_later, ahead)
    z2, z3 = sent_rep(c2, dz=2), sent_rep(c3, dz=3)
    c1, x_sib = together(c1, x_sib)
    z1 = sent_rep(c1, dz=1)
    far_y, b, near_o = part_sums("first", [(2, [], False), (4, [], False), (2, [], False)])
    w, w_s, f1, f2, v, far_y, b, near_o, z1, z3, z2 = together(w, w_s, f1, f2, v, far_y, b, near_o, z1, z3, z2)

    b, f3, far_y = sent(b, behind), sent(f1, ahead), sent(far_y, to_y)
    d1, d2 = sent(f1, to_core), sent(f2, to_core)
    v_later, f1, d1 = together(v, f1, d1)
    v_s = sent(v_later, to_core)
    snap = group_columns(snapshot, gz, gh, width).astype(jnp.float32)
    total = snap - group_columns(w, gz, gh, width).astype(jnp.float32)
    for part in (z1, z3, z2):
        total = total + (snap - part.astype(jnp.float32))
    total, f2, d2 = together(total, f2, d2)
    total_in = sent_rep(total[rows:], dh=1)
    grad = columns("grad1", [(w, 0), (w_s, 0), (f1, 0), (f2, 0)], None)
    (far,) = part_sums("far", [(2, [0], False)], [(far_y, lambda i, at: i)])
    b, f3, d1, d2, v, v_s, total, total_in, grad, far, near_o = together(
        b, f3, d1, d2, v, v_s, total, total_in, grad, far, near_o
    )

    far, near_o, h, d3 = sent(far, ahead), sent(near_o, ahead), sent(f3, to_y), sent(f3, to_core)
    outer_grad = (total[:rows] + total_in) / groups
    new_momentum = outer_beta * momentum + outer_grad
    new_part = snap[:rows] - outer_rate * (outer_grad + outer_beta * new_momentum)
    part_in = sent_rep(new_part, dh=1)
    grad = columns("grad2", [(d1, 0), (d2, 0), (v, 0), (v_s, 0)], grad)
    v_later, far, grad = together(v, far, grad)
    g1 = sent(v_later, ahead)
    near, home_o = part_sums(
        "near",
        [(2, [0], False), (2, [1, 2], False)],
        [
            (far, lambda i, at: jnp.clip(i, 0, 1)),
            (b, lambda i, at: jnp.clip(i, 2, 3)),
            (near_o, lambda i, at: jnp.clip(i - 2, 0, 1)),
        ],
    )
    near, home_o, h, f3, d3, v_s, g1, b, new_momentum, new_part, part_in, grad = together(
        near, home_o, h, f3, d3, v_s, g1, b, new_momentum, new_part, part_in, grad
    )

    near, from_y, g2, e1 = sent(near, ahead), sent(home_o, to_y), sent(v_s, ahead), sent(g1, to_core)
    part = jnp.concatenate([new_part, part_in], axis=0)
    z1 = sent_rep(part, dz=1)
    part_later, e1 = together(part, e1)
    z3 = sent_rep(part_later, dz=3)
    grad = columns("grad3", [(f3, 0), (d3, 0), (h, 0), (g1, 0), (e1, 0)], grad)
    by_core = [(array, lambda i, at: at[starts["cores"] + i]) for array in (b, near, from_y)]
    for_other, weight_grad = part_sums(
        "home", [(1, [0, 1, 2], False), (1, [0, 1, 2], True)], by_core, final_at=starts["cores"] + 1
    )
    h, g2, part, z1, z3, grad, for_other, weight_grad = together(h, g2, part, z1, z3, grad, for_other, weight_grad)

    from_other, e2, h_s = sent(for_other, to_core), sent(g2, to_core), sent(h, to_core)
    z2 = sent_rep(z1, dz=1)
    weight_grad = last_rows(at, starts["cores"], from_other, weight_grad)
    input_grad = columns("grad4", [(h_s, 0), (g2, 0), (e2, 0)], grad)
    rep_at, _ = together(rep_at, input_grad)
    new_weights = assembled([part, z1, z3, z2], rep_at)
    return input_grad, weight_grad[None], new_weights, new_momentum


def solution(mesh):
    return jax.shard_map(
        per_device,
        mesh=mesh,
        in_specs=(
            P(("rep", "fsdp")),
            P(("rep", "fsdp"), None),
            P(("rep", "fsdp"), None),
            P("rep", "fsdp", None),
            P("fsdp", None),
            P("fsdp", "rep"),
        ),
        out_specs=(
            P(("rep", "fsdp"), None),
            P("rep", "fsdp", None),
            P("fsdp", None),
            P("fsdp", "rep"),
        ),
        check_vma=False,
    )
```

```python
import jax
import jax.numpy as jnp
import numpy as np
from jax import lax
from jax.experimental import pallas as pl
from jax.experimental.pallas import tpu as pltpu
from jax.sharding import PartitionSpec as P

outer_rate = 0.7
outer_beta = 0.9
top_code = 32767.0
group_rows = 64
half = 256
MB = 1 << 20
vmem = 60 * MB
tiny = pl.CostEstimate(flops=1000, bytes_accessed=1000, transcendentals=0)


def fsdp_index(y, x, c):
    return y * 8 + x * 2 + c


def decoded(ref):
    rows = ref.shape[1] * group_rows // (group_rows + 1)
    codes = ref[0, :rows, :].astype(jnp.int32).astype(jnp.float32)
    unit = jnp.exp2(ref[0, rows:, :].astype(jnp.int32).astype(jnp.float32) * 0.25) * (1.0 / top_code)
    groups, width = unit.shape
    return (codes.reshape(groups, group_rows, width) * unit[:, None, :]).reshape(rows, width)


def store_coded(out_ref, total):
    rows, width = total.shape
    grouped = total.reshape(rows // group_rows, group_rows, width)
    peak = jnp.maximum(jnp.max(jnp.abs(grouped), axis=1), 1e-33)
    exponent = jnp.ceil(4.0 * jnp.log2(peak) + 0.01)
    scale = top_code / jnp.exp2(exponent * 0.25)
    codes = jnp.round(grouped * scale[:, None, :]).astype(jnp.int32).astype(jnp.int16)
    out_ref[0, :rows, :] = codes.reshape(rows, width)
    out_ref[0, rows:, :] = exponent.astype(jnp.int32).astype(jnp.int16)


def sums_kernel(groups, n_adds, at_ref, mt_ref, own_ref, sib_ref, *refs):
    step = pl.program_id(0)
    adds, outs = refs[:n_adds], refs[-len(groups) :]
    first = 0
    for (count, used, final), out_ref in zip(groups, outs, strict=True):

        @pl.when((step >= first) & (step < first + count))
        def _(used=used, final=final, out_ref=out_ref):
            tokens = jnp.concatenate([own_ref[...], sib_ref[...]], axis=0)
            total = jnp.dot(mt_ref[...], tokens, preferred_element_type=jnp.float32)
            for j in used:
                total = total + decoded(adds[j])
            if final:
                out_ref[...] = total.T
            else:
                store_coded(out_ref, total)

        first += count


def sums(at, offset, mt, x_own, x_sib, groups, adds=(), final_at=0):
    rows, both_tokens = mt.shape
    tokens = both_tokens // 2
    coded = rows + rows // group_rows
    specs = [
        pl.BlockSpec(mt.shape, lambda i, at: (0, 0)),
        pl.BlockSpec((tokens, half), lambda i, at: (0, at[offset + i])),
        pl.BlockSpec((tokens, half), lambda i, at: (0, at[offset + i])),
    ]
    for _, index in adds:
        specs.append(pl.BlockSpec((1, coded, half), lambda i, at, index=index: (index(i, at), 0, 0)))
    out_specs, out_shapes, first = [], [], 0
    for count, _, final in groups:
        if final:
            out_specs.append(pl.BlockSpec((half, rows), lambda i, at: (at[final_at], 0)))
            out_shapes.append(jax.ShapeDtypeStruct((2 * half, rows), jnp.float32))
        else:
            out_specs.append(
                pl.BlockSpec(
                    (1, coded, half),
                    lambda i, at, first=first, count=count: (jnp.clip(i - first, 0, count - 1), 0, 0),
                )
            )
            out_shapes.append(jax.ShapeDtypeStruct((count, coded, half), jnp.int16))
        first += count
    return pl.pallas_call(
        lambda *refs: sums_kernel(groups, len(adds), *refs),
        grid_spec=pltpu.PrefetchScalarGridSpec(
            num_scalar_prefetch=1, grid=(first,), in_specs=specs, out_specs=out_specs
        ),
        out_shape=out_shapes,
        compiler_params=pltpu.CompilerParams(vmem_limit_bytes=vmem),
        cost_estimate=tiny,
        name="partial_sums",
    )(at, mt, x_own, x_sib, *[array for array, _ in adds])


def last_kernel(at_ref, add_ref, _, out_ref):
    out_ref[...] = decoded(add_ref).T


def last_rows(at, offset, coded, so_far):
    return pl.pallas_call(
        last_kernel,
        grid_spec=pltpu.PrefetchScalarGridSpec(
            num_scalar_prefetch=1,
            grid=(1,),
            in_specs=[pl.BlockSpec(coded.shape, lambda i, at: (0, 0, 0)), pl.BlockSpec(memory_space=pl.ANY)],
            out_specs=pl.BlockSpec((half, so_far.shape[1]), lambda i, at: (at[offset], 0)),
        ),
        out_shape=jax.ShapeDtypeStruct(so_far.shape, so_far.dtype),
        input_output_aliases={2: 0},
        compiler_params=pltpu.CompilerParams(vmem_limit_bytes=vmem),
        cost_estimate=tiny,
        name="last_rows",
    )(at, coded, so_far)


def columns_kernel(n, at_ref, masked_ref, *refs):
    step = pl.program_id(0)
    out_ref = refs[-1]
    for j in range(n):

        @pl.when(step == j)
        def _(piece=refs[j]):
            out_ref[...] = lax.dot_general(
                masked_ref[...], piece[...], (((1,), (1,)), ((), ())), preferred_element_type=jnp.float32
            )


def grad_columns(at, offset, masked, pieces, wide, so_far, rows):
    n = len(pieces)
    features = pieces[0][0].shape[1]
    tokens = masked.shape[0]
    specs = [pl.BlockSpec(masked.shape, lambda i, at: (0, 0))]
    specs += [pl.BlockSpec((rows, features), lambda i, at, k=k: (k, 0)) for _, k in pieces]
    operands = [at, masked, *[array for array, _ in pieces]]
    aliases = {}
    if so_far is not None:
        specs.append(pl.BlockSpec(memory_space=pl.ANY))
        aliases = {len(operands): 0}
        operands.append(so_far)
    return pl.pallas_call(
        lambda *refs: columns_kernel(n, *refs),
        grid_spec=pltpu.PrefetchScalarGridSpec(
            num_scalar_prefetch=1,
            grid=(n,),
            in_specs=specs,
            out_specs=pl.BlockSpec((tokens, rows), lambda i, at: (0, at[offset + i])),
        ),
        out_shape=jax.ShapeDtypeStruct((tokens, wide), jnp.float32),
        input_output_aliases=aliases,
        compiler_params=pltpu.CompilerParams(vmem_limit_bytes=vmem),
        cost_estimate=tiny,
        name="grad_columns",
    )(*operands)


def transpose_kernel(own_ref, sib_ref, out_ref):
    tokens = own_ref.shape[0]
    out_ref[:, :tokens] = own_ref[...].T
    out_ref[:, tokens:] = sib_ref[...].T


def transposed(own, sib):
    tokens, features = own.shape
    return pl.pallas_call(
        transpose_kernel,
        grid=(1,),
        in_specs=[pl.BlockSpec(own.shape, lambda i: (0, 0))] * 2,
        out_specs=pl.BlockSpec((features, 2 * tokens), lambda i: (0, 0)),
        out_shape=jax.ShapeDtypeStruct((features, 2 * tokens), own.dtype),
        compiler_params=pltpu.CompilerParams(vmem_limit_bytes=vmem),
        cost_estimate=tiny,
        name="transposed",
    )(own, sib)


def assemble_kernel(at_ref, *refs):
    out_ref = refs[-1]
    for k, piece in enumerate(refs[:-1]):
        width = piece.shape[1]
        out_ref[:, pl.ds(pl.multiple_of(at_ref[k] * width, width), width)] = piece[...]


def assembled(pieces, places):
    both_rows, width = pieces[0].shape
    rows, steps = both_rows // 2, 4
    tile = rows // steps
    return pl.pallas_call(
        assemble_kernel,
        grid_spec=pltpu.PrefetchScalarGridSpec(
            num_scalar_prefetch=1,
            grid=(steps,),
            in_specs=[pl.BlockSpec((tile, width), lambda i, at, k=k: (k * steps + i, 0)) for _ in pieces for k in range(2)],
            out_specs=pl.BlockSpec((tile, 8 * width), lambda i, at: (i, 0)),
        ),
        out_shape=jax.ShapeDtypeStruct((rows, 8 * width), jnp.float32),
        compiler_params=pltpu.CompilerParams(vmem_limit_bytes=vmem),
        cost_estimate=tiny,
        name="assembled",
    )(places, *[piece for piece in pieces for _ in range(2)])


def group_columns(array, zz, h, width):
    cut = lambda hh: lax.dynamic_slice_in_dim(array, (hh * 4 + zz) * width, width, 1)
    return jnp.concatenate([cut(h), cut(1 - h)], axis=0)


def together(*arrays):
    return lax.optimization_barrier(arrays)


def sent(array, pairs):
    return lax.ppermute(array, "fsdp", pairs)


def sent_rep(array, dh=0, dz=0):
    pairs = [(h * 4 + z, (h ^ dh) * 4 + (z + dz) % 4) for h in range(2) for z in range(4)]
    return lax.ppermute(array, "rep", pairs)


chips = [(y, x, c) for y in range(2) for x in range(4) for c in range(2)]
to_core = [(fsdp_index(y, x, c), fsdp_index(y, x, 1 - c)) for y, x, c in chips]
to_y = [(fsdp_index(y, x, c), fsdp_index(1 - y, x, c)) for y, x, c in chips]
ahead = [(fsdp_index(y, x, c), fsdp_index(y, (x + 1 - 2 * c) % 4, c)) for y, x, c in chips]
behind = [(fsdp_index(y, x, c), fsdp_index(y, (x - 1 + 2 * c) % 4, c)) for y, x, c in chips]


def tables():
    starts, rows = {}, []
    for me in range(16):
        y, x, c = me // 8, (me // 2) % 4, me % 2
        s, o, row = 1 - 2 * c, 1 - c, []

        def cols(yy, dx):
            return [fsdp_index(yy, (x + dx) % 4, cc) * 2 + c for cc in range(2)]

        def places(*pieces):
            return [fsdp_index(y ^ dy, (x + dx) % 4, cc) for dy, dx, cc in pieces]

        for name, entries in (
            ("first", cols(1 - y, 2) + cols(y, -s) + cols(1 - y, -s) + cols(1 - y, s)),
            ("far", cols(y, 2)),
            ("near", cols(y, s) + cols(1 - y, 0)),
            ("home", [fsdp_index(y, x, cc) * 2 + c for cc in (o, c)]),
            ("cores", [o, c]),
            ("grad1", places((0, 0, c), (0, 0, o), (0, -s, c), (0, -s, o))),
            ("grad2", places((0, s, o), (0, s, c), (1, 0, c), (1, 0, o))),
            ("grad3", places((0, 2, c), (0, 2, o), (1, 2, c), (1, -s, c), (1, s, o))),
            ("grad4", places((1, 2, o), (1, -s, o), (1, s, c))),
        ):
            starts[name] = len(row)
            row += entries
        rows.append(row)
    rep_rows = []
    for me in range(8):
        h, z = me // 4, me % 4
        rep_rows.append([hh * 4 + (z - dz) % 4 for dz in (0, 1, 3, 2) for hh in (h, 1 - h)])
    return starts, np.array(rows, np.int32), np.array(rep_rows, np.int32)


def per_device(token_ids, normed_inputs, kv_cotangent, replica_weights, snapshot, momentum):
    wide = normed_inputs.shape[1]
    w = replica_weights[0]
    block = w.shape[0]
    groups = lax.axis_size("rep")
    rep = lax.axis_index("rep")
    gh, gz = rep // 4, rep % 4
    rows, width = momentum.shape
    starts, table, rep_table = tables()
    at = lax.dynamic_index_in_dim(jnp.asarray(table), lax.axis_index("fsdp"), 0, keepdims=False)
    rep_at = lax.dynamic_index_in_dim(jnp.asarray(rep_table), rep, 0, keepdims=False)

    def columns(name, pieces, so_far):
        return grad_columns(at, starts[name], masked, pieces, wide, so_far, block)

    def part_sums(name, *args, **kw):
        return sums(at, starts[name], mt, normed_inputs, x_sib, *args, **kw)

    x_sib = sent(normed_inputs, to_core)
    f1, v, w_s = sent(w, ahead), sent(w, to_y), sent(w, to_core)
    live_rows = (token_ids != 0).astype(jnp.bfloat16)[:, None]
    masked = kv_cotangent * live_rows
    masked_sib = sent(masked, to_core)
    mt = transposed(masked, masked_sib)
    w_z, masked_sib, w_s = together(w, masked_sib, w_s)
    c1, c2, c3 = (group_columns(w_z, (gz + dz) % 4, gh, width) for dz in (1, 2, 3))
    w_later, x_sib, mt, at, rep_at, c1, c2, c3 = together(w_s, x_sib, mt, at, rep_at, c1, c2, c3)
    f2, z2, z3 = sent(w_later, ahead), sent_rep(c2, dz=2), sent_rep(c3, dz=3)
    c1, f1 = together(c1, f1)
    z1 = sent_rep(c1, dz=1)
    far_y, b, near_o = part_sums("first", [(2, [], False), (4, [], False), (2, [], False)])
    w, w_s, f1, f2, v, far_y, b, near_o, z1, z3, z2 = together(w, w_s, f1, f2, v, far_y, b, near_o, z1, z3, z2)

    b, f3, far_y = sent(b, behind), sent(f1, ahead), sent(far_y, to_y)
    d1, d2 = sent(f1, to_core), sent(f2, to_core)
    v_later, f1, d1 = together(v, f1, d1)
    v_s = sent(v_later, to_core)
    snap = group_columns(snapshot, gz, gh, width).astype(jnp.float32)
    total = snap - group_columns(w, gz, gh, width).astype(jnp.float32)
    for part in (z1, z3, z2):
        total = total + (snap - part.astype(jnp.float32))
    total, f2, d2 = together(total, f2, d2)
    total_in = sent_rep(total[rows:], dh=1)
    grad = columns("grad1", [(w, 0), (w_s, 0), (f1, 0), (f2, 0)], None)
    (far,) = part_sums("far", [(2, [0], False)], [(far_y, lambda i, at: i)])
    b, f3, d1, d2, v, v_s, total, total_in, grad, far, near_o = together(
        b, f3, d1, d2, v, v_s, total, total_in, grad, far, near_o
    )

    far, near_o, h, d3 = sent(far, ahead), sent(near_o, ahead), sent(f3, to_y), sent(f3, to_core)
    outer_grad = (total[:rows] + total_in) / groups
    new_momentum = outer_beta * momentum + outer_grad
    new_part = snap[:rows] - outer_rate * (outer_grad + outer_beta * new_momentum)
    part_in = sent_rep(new_part, dh=1)
    grad = columns("grad2", [(d1, 0), (d2, 0), (v, 0), (v_s, 0)], grad)
    v_later, far, grad = together(v, far, grad)
    g1 = sent(v_later, ahead)
    near, home_o = part_sums(
        "near",
        [(2, [0], False), (2, [1, 2], False)],
        [
            (far, lambda i, at: jnp.clip(i, 0, 1)),
            (b, lambda i, at: jnp.clip(i, 2, 3)),
            (near_o, lambda i, at: jnp.clip(i - 2, 0, 1)),
        ],
    )
    near, home_o, h, f3, d3, v_s, g1, b, new_momentum, new_part, part_in, grad = together(
        near, home_o, h, f3, d3, v_s, g1, b, new_momentum, new_part, part_in, grad
    )

    near, from_y, g2, e1 = sent(near, ahead), sent(home_o, to_y), sent(v_s, ahead), sent(g1, to_core)
    part = jnp.concatenate([new_part, part_in], axis=0)
    z1 = sent_rep(part, dz=1)
    part_later, e1 = together(part, e1)
    z3 = sent_rep(part_later, dz=3)
    grad = columns("grad3", [(f3, 0), (d3, 0), (h, 0), (g1, 0), (e1, 0)], grad)
    by_core = [(array, lambda i, at: at[starts["cores"] + i]) for array in (b, near, from_y)]
    for_other, weight_grad = part_sums(
        "home", [(1, [0, 1, 2], False), (1, [0, 1, 2], True)], by_core, final_at=starts["cores"] + 1
    )
    h, g2, part, z1, z3, grad, for_other, weight_grad = together(h, g2, part, z1, z3, grad, for_other, weight_grad)

    from_other, e2, h_s = sent(for_other, to_core), sent(g2, to_core), sent(h, to_core)
    z2 = sent_rep(z1, dz=1)
    weight_grad = last_rows(at, starts["cores"], from_other, weight_grad)
    input_grad = columns("grad4", [(h_s, 0), (g2, 0), (e2, 0)], grad)
    rep_at, _ = together(rep_at, input_grad)
    new_weights = assembled([part, z1, z3, z2], rep_at)
    return input_grad, weight_grad[None], new_weights, new_momentum


def solution(mesh):
    return jax.shard_map(
        per_device,
        mesh=mesh,
        in_specs=(
            P(("rep", "fsdp")),
            P(("rep", "fsdp"), None),
            P(("rep", "fsdp"), None),
            P("rep", "fsdp", None),
            P("fsdp", None),
            P("fsdp", "rep"),
        ),
        out_specs=(
            P(("rep", "fsdp"), None),
            P("rep", "fsdp", None),
            P("fsdp", None),
            P("fsdp", "rep"),
        ),
        check_vma=False,
    )
```

```python
import jax
import jax.numpy as jnp
import numpy as np
from jax import lax
from jax.experimental import pallas as pl
from jax.experimental.pallas import tpu as pltpu
from jax.sharding import PartitionSpec as P

outer_rate = 0.7
outer_beta = 0.9
top_code = 32767.0
group_rows = 64
half = 256
MB = 1 << 20
vmem = 28 * MB
tiny = pl.CostEstimate(flops=1000, bytes_accessed=1000, transcendentals=0)


def fsdp_index(y, x, c):
    return y * 8 + x * 2 + c


def decoded(ref):
    rows = ref.shape[1] * group_rows // (group_rows + 1)
    codes = ref[0, :rows, :].astype(jnp.int32).astype(jnp.float32)
    unit = jnp.exp2(ref[0, rows:, :].astype(jnp.int32).astype(jnp.float32) * 0.25) * (1.0 / top_code)
    groups, width = unit.shape
    return (codes.reshape(groups, group_rows, width) * unit[:, None, :]).reshape(rows, width)


def store_coded(out_ref, total):
    rows, width = total.shape
    grouped = total.reshape(rows // group_rows, group_rows, width)
    peak = jnp.maximum(jnp.max(jnp.abs(grouped), axis=1), 1e-33)
    exponent = jnp.ceil(4.0 * jnp.log2(peak) + 0.01)
    scale = top_code / jnp.exp2(exponent * 0.25)
    codes = jnp.round(grouped * scale[:, None, :]).astype(jnp.int32).astype(jnp.int16)
    out_ref[0, :rows, :] = codes.reshape(rows, width)
    out_ref[0, rows:, :] = exponent.astype(jnp.int32).astype(jnp.int16)


def sums_kernel(groups, n_adds, at_ref, mt_ref, own_ref, sib_ref, *refs):
    step = pl.program_id(0)
    adds, outs = refs[:n_adds], refs[-len(groups) :]
    first = 0
    for (count, used, final), out_ref in zip(groups, outs, strict=True):

        @pl.when((step >= first) & (step < first + count))
        def _(used=used, final=final, out_ref=out_ref):
            tokens = jnp.concatenate([own_ref[...], sib_ref[...]], axis=0)
            total = jnp.dot(mt_ref[...], tokens, preferred_element_type=jnp.float32)
            for j in used:
                total = total + decoded(adds[j])
            if final:
                out_ref[...] = total.T
            else:
                store_coded(out_ref, total)

        first += count


def sums(at, offset, mt, x_own, x_sib, groups, adds=(), final_at=0):
    rows, both_tokens = mt.shape
    tokens = both_tokens // 2
    coded = rows + rows // group_rows
    specs = [
        pl.BlockSpec(mt.shape, lambda i, at: (0, 0)),
        pl.BlockSpec((tokens, half), lambda i, at: (0, at[offset + i])),
        pl.BlockSpec((tokens, half), lambda i, at: (0, at[offset + i])),
    ]
    for _, index in adds:
        specs.append(pl.BlockSpec((1, coded, half), lambda i, at, index=index: (index(i, at), 0, 0)))
    out_specs, out_shapes, first = [], [], 0
    for count, _, final in groups:
        if final:
            out_specs.append(pl.BlockSpec((half, rows), lambda i, at: (at[final_at], 0)))
            out_shapes.append(jax.ShapeDtypeStruct((2 * half, rows), jnp.float32))
        else:
            out_specs.append(
                pl.BlockSpec(
                    (1, coded, half),
                    lambda i, at, first=first, count=count: (jnp.clip(i - first, 0, count - 1), 0, 0),
                )
            )
            out_shapes.append(jax.ShapeDtypeStruct((count, coded, half), jnp.int16))
        first += count
    return pl.pallas_call(
        lambda *refs: sums_kernel(groups, len(adds), *refs),
        grid_spec=pltpu.PrefetchScalarGridSpec(
            num_scalar_prefetch=1, grid=(first,), in_specs=specs, out_specs=out_specs
        ),
        out_shape=out_shapes,
        compiler_params=pltpu.CompilerParams(vmem_limit_bytes=vmem),
        cost_estimate=tiny,
        name="partial_sums",
    )(at, mt, x_own, x_sib, *[array for array, _ in adds])


def last_kernel(at_ref, add_ref, _, out_ref):
    out_ref[...] = decoded(add_ref).T


def last_rows(at, offset, coded, so_far):
    return pl.pallas_call(
        last_kernel,
        grid_spec=pltpu.PrefetchScalarGridSpec(
            num_scalar_prefetch=1,
            grid=(1,),
            in_specs=[pl.BlockSpec(coded.shape, lambda i, at: (0, 0, 0)), pl.BlockSpec(memory_space=pl.ANY)],
            out_specs=pl.BlockSpec((half, so_far.shape[1]), lambda i, at: (at[offset], 0)),
        ),
        out_shape=jax.ShapeDtypeStruct(so_far.shape, so_far.dtype),
        input_output_aliases={2: 0},
        compiler_params=pltpu.CompilerParams(vmem_limit_bytes=vmem),
        cost_estimate=tiny,
        name="last_rows",
    )(at, coded, so_far)


def columns_kernel(n, at_ref, masked_ref, *refs):
    step = pl.program_id(0)
    out_ref = refs[-1]
    for j in range(n):

        @pl.when(step == j)
        def _(piece=refs[j]):
            out_ref[...] = lax.dot_general(
                masked_ref[...], piece[...], (((1,), (1,)), ((), ())), preferred_element_type=jnp.float32
            )


def grad_columns(at, offset, masked, pieces, wide, so_far, rows):
    n = len(pieces)
    features = pieces[0][0].shape[1]
    tokens = masked.shape[0]
    specs = [pl.BlockSpec(masked.shape, lambda i, at: (0, 0))]
    specs += [pl.BlockSpec((rows, features), lambda i, at, k=k: (k, 0)) for _, k in pieces]
    operands = [at, masked, *[array for array, _ in pieces]]
    aliases = {}
    if so_far is not None:
        specs.append(pl.BlockSpec(memory_space=pl.ANY))
        aliases = {len(operands): 0}
        operands.append(so_far)
    return pl.pallas_call(
        lambda *refs: columns_kernel(n, *refs),
        grid_spec=pltpu.PrefetchScalarGridSpec(
            num_scalar_prefetch=1,
            grid=(n,),
            in_specs=specs,
            out_specs=pl.BlockSpec((tokens, rows), lambda i, at: (0, at[offset + i])),
        ),
        out_shape=jax.ShapeDtypeStruct((tokens, wide), jnp.float32),
        input_output_aliases=aliases,
        compiler_params=pltpu.CompilerParams(vmem_limit_bytes=vmem),
        cost_estimate=tiny,
        name="grad_columns",
    )(*operands)


def transpose_kernel(own_ref, sib_ref, out_ref):
    tokens = own_ref.shape[0]
    out_ref[:, :tokens] = own_ref[...].T
    out_ref[:, tokens:] = sib_ref[...].T


def transposed(own, sib):
    tokens, features = own.shape
    return pl.pallas_call(
        transpose_kernel,
        grid=(1,),
        in_specs=[pl.BlockSpec(own.shape, lambda i: (0, 0))] * 2,
        out_specs=pl.BlockSpec((features, 2 * tokens), lambda i: (0, 0)),
        out_shape=jax.ShapeDtypeStruct((features, 2 * tokens), own.dtype),
        compiler_params=pltpu.CompilerParams(vmem_limit_bytes=vmem),
        cost_estimate=tiny,
        name="transposed",
    )(own, sib)


def assemble_kernel(at_ref, *refs):
    out_ref = refs[-1]
    for k, piece in enumerate(refs[:-1]):
        width = piece.shape[1]
        out_ref[:, pl.ds(pl.multiple_of(at_ref[k] * width, width), width)] = piece[...]


def assembled(pieces, places):
    both_rows, width = pieces[0].shape
    rows, steps = both_rows // 2, 4
    tile = rows // steps
    return pl.pallas_call(
        assemble_kernel,
        grid_spec=pltpu.PrefetchScalarGridSpec(
            num_scalar_prefetch=1,
            grid=(steps,),
            in_specs=[pl.BlockSpec((tile, width), lambda i, at, k=k: (k * steps + i, 0)) for _ in pieces for k in range(2)],
            out_specs=pl.BlockSpec((tile, 8 * width), lambda i, at: (i, 0)),
        ),
        out_shape=jax.ShapeDtypeStruct((rows, 8 * width), jnp.float32),
        compiler_params=pltpu.CompilerParams(vmem_limit_bytes=vmem),
        cost_estimate=tiny,
        name="assembled",
    )(places, *[piece for piece in pieces for _ in range(2)])


def group_columns(array, zz, h, width):
    cut = lambda hh: lax.dynamic_slice_in_dim(array, (hh * 4 + zz) * width, width, 1)
    return jnp.concatenate([cut(h), cut(1 - h)], axis=0)


def together(*arrays):
    return lax.optimization_barrier(arrays)


def sent(array, pairs):
    return lax.ppermute(array, "fsdp", pairs)


def sent_rep(array, dh=0, dz=0):
    pairs = [(h * 4 + z, (h ^ dh) * 4 + (z + dz) % 4) for h in range(2) for z in range(4)]
    return lax.ppermute(array, "rep", pairs)


chips = [(y, x, c) for y in range(2) for x in range(4) for c in range(2)]
to_core = [(fsdp_index(y, x, c), fsdp_index(y, x, 1 - c)) for y, x, c in chips]
to_y = [(fsdp_index(y, x, c), fsdp_index(1 - y, x, c)) for y, x, c in chips]
ahead = [(fsdp_index(y, x, c), fsdp_index(y, (x + 1 - 2 * c) % 4, c)) for y, x, c in chips]
behind = [(fsdp_index(y, x, c), fsdp_index(y, (x - 1 + 2 * c) % 4, c)) for y, x, c in chips]


def tables():
    starts, rows = {}, []
    for me in range(16):
        y, x, c = me // 8, (me // 2) % 4, me % 2
        s, o, row = 1 - 2 * c, 1 - c, []

        def cols(yy, dx):
            return [fsdp_index(yy, (x + dx) % 4, cc) * 2 + c for cc in range(2)]

        def places(*pieces):
            return [fsdp_index(y ^ dy, (x + dx) % 4, cc) for dy, dx, cc in pieces]

        for name, entries in (
            ("first", cols(1 - y, 2) + cols(y, -s) + cols(1 - y, -s) + cols(1 - y, s)),
            ("far", cols(y, 2)),
            ("near", cols(y, s) + cols(1 - y, 0)),
            ("home", [fsdp_index(y, x, cc) * 2 + c for cc in (o, c)]),
            ("cores", [o, c]),
            ("grad1", places((0, 0, c), (0, 0, o), (0, -s, c), (0, -s, o))),
            ("grad2", places((0, s, o), (0, s, c), (1, 0, c), (1, 0, o))),
            ("grad3", places((0, 2, c), (0, 2, o), (1, 2, c), (1, -s, c), (1, s, o))),
            ("grad4", places((1, 2, o), (1, -s, o), (1, s, c))),
        ):
            starts[name] = len(row)
            row += entries
        rows.append(row)
    rep_rows = []
    for me in range(8):
        h, z = me // 4, me % 4
        rep_rows.append([hh * 4 + (z - dz) % 4 for dz in (0, 1, 3, 2) for hh in (h, 1 - h)])
    return starts, np.array(rows, np.int32), np.array(rep_rows, np.int32)


def per_device(token_ids, normed_inputs, kv_cotangent, replica_weights, snapshot, momentum):
    wide = normed_inputs.shape[1]
    w = replica_weights[0]
    block = w.shape[0]
    groups = lax.axis_size("rep")
    rep = lax.axis_index("rep")
    gh, gz = rep // 4, rep % 4
    rows, width = momentum.shape
    starts, table, rep_table = tables()
    at = lax.dynamic_index_in_dim(jnp.asarray(table), lax.axis_index("fsdp"), 0, keepdims=False)
    rep_at = lax.dynamic_index_in_dim(jnp.asarray(rep_table), rep, 0, keepdims=False)

    def columns(name, pieces, so_far):
        return grad_columns(at, starts[name], masked, pieces, wide, so_far, block)

    def part_sums(name, *args, **kw):
        return sums(at, starts[name], mt, normed_inputs, x_sib, *args, **kw)

    x_sib = sent(normed_inputs, to_core)
    f1, v, w_s = sent(w, ahead), sent(w, to_y), sent(w, to_core)
    live_rows = (token_ids != 0).astype(jnp.bfloat16)[:, None]
    masked = kv_cotangent * live_rows
    masked_sib = sent(masked, to_core)
    mt = transposed(masked, masked_sib)
    w_z, masked_sib, w_s = together(w, masked_sib, w_s)
    c1, c2, c3 = (group_columns(w_z, (gz + dz) % 4, gh, width) for dz in (1, 2, 3))
    w_later, x_sib, mt, at, rep_at, c1, c2, c3 = together(w_s, x_sib, mt, at, rep_at, c1, c2, c3)
    f2, z2, z3 = sent(w_later, ahead), sent_rep(c2, dz=2), sent_rep(c3, dz=3)
    c1, f1 = together(c1, f1)
    z1 = sent_rep(c1, dz=1)
    far_y, b, near_o = part_sums("first", [(2, [], False), (4, [], False), (2, [], False)])
    w, w_s, f1, f2, v, far_y, b, near_o, z1, z3, z2 = together(w, w_s, f1, f2, v, far_y, b, near_o, z1, z3, z2)

    b, f3, far_y = sent(b, behind), sent(f1, ahead), sent(far_y, to_y)
    d1, d2 = sent(f1, to_core), sent(f2, to_core)
    v_later, f1, d1 = together(v, f1, d1)
    v_s = sent(v_later, to_core)
    snap = group_columns(snapshot, gz, gh, width).astype(jnp.float32)
    total = snap - group_columns(w, gz, gh, width).astype(jnp.float32)
    for part in (z1, z3, z2):
        total = total + (snap - part.astype(jnp.float32))
    total, f2, d2 = together(total, f2, d2)
    total_in = sent_rep(total[rows:], dh=1)
    grad = columns("grad1", [(w, 0), (w_s, 0), (f1, 0), (f2, 0)], None)
    (far,) = part_sums("far", [(2, [0], False)], [(far_y, lambda i, at: i)])
    b, f3, d1, d2, v, v_s, total, total_in, grad, far, near_o = together(
        b, f3, d1, d2, v, v_s, total, total_in, grad, far, near_o
    )

    far, near_o, h, d3 = sent(far, ahead), sent(near_o, ahead), sent(f3, to_y), sent(f3, to_core)
    outer_grad = (total[:rows] + total_in) / groups
    new_momentum = outer_beta * momentum + outer_grad
    new_part = snap[:rows] - outer_rate * (outer_grad + outer_beta * new_momentum)
    part_in = sent_rep(new_part, dh=1)
    grad = columns("grad2", [(d1, 0), (d2, 0), (v, 0), (v_s, 0)], grad)
    v_later, far, grad = together(v, far, grad)
    g1 = sent(v_later, ahead)
    near, home_o = part_sums(
        "near",
        [(2, [0], False), (2, [1, 2], False)],
        [
            (far, lambda i, at: jnp.clip(i, 0, 1)),
            (b, lambda i, at: jnp.clip(i, 2, 3)),
            (near_o, lambda i, at: jnp.clip(i - 2, 0, 1)),
        ],
    )
    near, home_o, h, f3, d3, v_s, g1, b, new_momentum, new_part, part_in, grad = together(
        near, home_o, h, f3, d3, v_s, g1, b, new_momentum, new_part, part_in, grad
    )

    near, from_y, g2, e1 = sent(near, ahead), sent(home_o, to_y), sent(v_s, ahead), sent(g1, to_core)
    part = jnp.concatenate([new_part, part_in], axis=0)
    z1 = sent_rep(part, dz=1)
    part_later, e1 = together(part, e1)
    z3 = sent_rep(part_later, dz=3)
    grad = columns("grad3", [(f3, 0), (d3, 0), (h, 0), (g1, 0), (e1, 0)], grad)
    by_core = [(array, lambda i, at: at[starts["cores"] + i]) for array in (b, near, from_y)]
    for_other, weight_grad = part_sums(
        "home", [(1, [0, 1, 2], False), (1, [0, 1, 2], True)], by_core, final_at=starts["cores"] + 1
    )
    h, g2, part, z1, z3, grad, for_other, weight_grad = together(h, g2, part, z1, z3, grad, for_other, weight_grad)

    from_other, e2, h_s = sent(for_other, to_core), sent(g2, to_core), sent(h, to_core)
    z2 = sent_rep(z1, dz=1)
    weight_grad = last_rows(at, starts["cores"], from_other, weight_grad)
    input_grad = columns("grad4", [(h_s, 0), (g2, 0), (e2, 0)], grad)
    rep_at, _ = together(rep_at, input_grad)
    new_weights = assembled([part, z1, z3, z2], rep_at)
    return input_grad, weight_grad[None], new_weights, new_momentum


def solution(mesh):
    return jax.shard_map(
        per_device,
        mesh=mesh,
        in_specs=(
            P(("rep", "fsdp")),
            P(("rep", "fsdp"), None),
            P(("rep", "fsdp"), None),
            P("rep", "fsdp", None),
            P("fsdp", None),
            P("fsdp", "rep"),
        ),
        out_specs=(
            P(("rep", "fsdp"), None),
            P("rep", "fsdp", None),
            P("fsdp", None),
            P("fsdp", "rep"),
        ),
        check_vma=False,
    )
```
